512 devices in a mesh: seg: 16 (over x, z_hi, core), blk: 4 (over y), uly: 8 (over z_lo).
Axes of the slice: x: 4, y: 4, z: 16 (z_hi: 2, z_lo: 8; z = z_hi * 8 + z_lo), core: 2. Of those that a mesh axis runs over, the one named last changes fastest.
Arguments:
- queries: bfloat16 [8192, 5120], P(('seg', 'blk', 'uly')), may hold values from -16 to 16
- keys: bfloat16 [8192, 5120], P(('seg', 'blk', 'uly')), may hold values from -16 to 16
- values: bfloat16 [8192, 5120], P(('seg', 'blk', 'uly')), may hold values from -6 to 6
- gain_q: float32 [5120], replicated, may hold values from 1.2 to 2.2
- gain_k: float32 [5120], replicated, may hold values from 1.2 to 2.2
- positions: int32 [3, 8192], P(None, ('seg', 'blk', 'uly')), may hold values from 0 to 51, as said below
- ref_group: int32 [16], replicated, may hold values from 0 to 15, each once
Outputs:
- attended: bfloat16 [8192, 5120], P(('seg', 'blk', 'uly'))
The draws below stay inside these ranges and needn't reach their ends.
Inputs may be any that keep to these rules, and one draw needn't show every extreme that they name: `positions`: frame below 21, row below 30, column below 52. `ref_group`: a permutation of the group numbers.
All inputs are finite; a program needn't handle non-finite values.
Results may differ from the reference program's by a relative error of at most 0.0095.
Values may be sent and summed in bfloat16 or wider, within the bound.
No kernel may reach another device: no remote copies, remote signals or barrier semaphores. Data moves between devices by JAX's collectives and lax.ppermute only.
A program may use at most 64 MiB of HBM per device.

```python
import jax
import jax.numpy as jnp
from jax import lax

HEADS = 40
HEAD_DIM = 128
GROUPS = 16
WIDTH = 5120
SEG_TOK = 512
TOKENS = 8192
N_SEG = 16


def draw_queries(key, part):
    key = jax.random.fold_in(key, 1)
    base = jax.random.normal(key, (TOKENS, WIDTH), jnp.float32)
    return jnp.clip(base, -16.0, 16.0).astype(jnp.bfloat16)


def draw_keys(key, part):
    key = jax.random.fold_in(key, 2)
    base = jax.random.normal(key, (TOKENS, WIDTH), jnp.float32)
    return jnp.clip(base, -16.0, 16.0).astype(jnp.bfloat16)


def draw_positions(key, part):
    key = jax.random.fold_in(key, 3)
    limits = jnp.array([21, 30, 52], jnp.int32)[:, None]
    raw_bits = jax.random.randint(key, (3, TOKENS), 0, 1 << 20)
    return raw_bits % limits


def shard_levels(key, dims, cuts, least, largest):
    loudness = 1.0
    for position, blocks in cuts:
        heights = jax.random.uniform(jax.random.fold_in(jax.random.fold_in(key, 6), position), (blocks,), jnp.float32, least / len(cuts), largest / len(cuts))
        loudness = loudness * jnp.repeat(jnp.exp(heights), dims[position] // blocks).reshape((-1,) + (1,) * (len(dims) - 1 - position))
    return loudness


def scatter_about(rng, shape, deviation, reach, cuts=(), kind=jnp.bfloat16):
    loudness = shard_levels(rng, shape, cuts, -0.22, 0.18) if cuts else 1.0
    drawn = jax.random.normal(rng, shape, jnp.float32) * deviation * loudness
    return jnp.minimum(jnp.maximum(drawn, -reach), reach).astype(kind)


def setup_inputs(seed: int = 0) -> dict:
    seeds = jax.random.split(jax.random.key(seed), 8)
    return {
        "queries": draw_queries(jax.random.fold_in(seeds[7], 71), 0),
        "keys": draw_keys(jax.random.fold_in(seeds[7], 71), 0),
        "values": scatter_about(seeds[2], (TOKENS, WIDTH), 1.0, 6.0, ((0, 512),)),
        "gain_q": jnp.clip(jax.random.uniform(seeds[3], (WIDTH,), jnp.float32, 1.2, 2.2), 1.2, 2.2),
        "gain_k": jnp.clip(jax.random.uniform(seeds[4], (WIDTH,), jnp.float32, 1.2, 2.2), 1.2, 2.2),
        "positions": draw_positions(jax.random.fold_in(seeds[7], 71), 0),
        "ref_group": jax.random.permutation(seeds[6], GROUPS).astype(jnp.int32),
    }


def norm_rows(source, gain):
    wide = source.astype(jnp.float32)
    mean_square = lax.optimization_barrier(jnp.mean(wide * wide, axis=-1, keepdims=True))
    return wide * lax.rsqrt(mean_square + 1e-06) * gain

def rope_angles(positions, head_dim):
    pair_count = head_dim // 2
    side_pairs = head_dim // 6
    time_pairs = pair_count - 2 * side_pairs

    def frequencies(number):
        return 1.0 / 10000.0 ** (jnp.arange(number, dtype=jnp.float32) * 2.0 / (2 * number))
    position_f = positions.astype(jnp.float32)
    angles = jnp.concatenate([position_f[0][:, None] * frequencies(time_pairs)[None, :], position_f[1][:, None] * frequencies(side_pairs)[None, :], position_f[2][:, None] * frequencies(side_pairs)[None, :]], axis=1)
    return (jnp.cos(angles), jnp.sin(angles))

def rotate(source, cos_table, sin_table, head_count, head_dim):
    token_count = source.shape[0]
    paired = source.reshape(token_count, head_count, head_dim // 2, 2)
    real_part = paired[..., 0]
    imag_part = paired[..., 1]
    cos_b = cos_table[:, None, :]
    sin_b = sin_table[:, None, :]
    turned = jnp.stack([real_part * cos_b - imag_part * sin_b, real_part * sin_b + imag_part * cos_b], axis=-1)
    return turned.reshape(token_count, head_count * head_dim)

def reference(queries, keys, values, gain_q, gain_k, positions, ref_group):
    cos_table, sin_table = rope_angles(positions, HEAD_DIM)
    q_rot = rotate(norm_rows(queries, gain_q), cos_table, sin_table, HEADS, HEAD_DIM).astype(jnp.bfloat16)
    k_rot = rotate(norm_rows(keys, gain_k), cos_table, sin_table, HEADS, HEAD_DIM).astype(jnp.bfloat16)
    q_groups = q_rot.reshape(N_SEG, SEG_TOK, HEADS, HEAD_DIM).transpose(0, 2, 1, 3)
    k_groups = k_rot.reshape(N_SEG, SEG_TOK, HEADS, HEAD_DIM).transpose(0, 2, 1, 3)
    v_groups = values.reshape(N_SEG, SEG_TOK, HEADS, HEAD_DIM).transpose(0, 2, 1, 3)
    group_ids = jnp.arange(ref_group.shape[0], dtype=jnp.int32)
    ref_index = jnp.sum(jnp.where(ref_group == 0, group_ids, 0)).astype(jnp.int32)
    ref_keys = lax.dynamic_index_in_dim(k_groups, ref_index, 0, keepdims=False)
    ref_values = lax.dynamic_index_in_dim(v_groups, ref_index, 0, keepdims=False)
    score_scale = HEAD_DIM ** (-0.5)

    def one_head(inputs):
        head_q, head_k, head_v = inputs
        scores = jnp.dot(head_q, head_k.T, preferred_element_type=jnp.float32) * score_scale
        weights = jnp.exp(scores - lax.optimization_barrier(jnp.max(scores, axis=-1, keepdims=True)))
        total = lax.optimization_barrier(jnp.sum(weights, axis=-1, keepdims=True))
        return jnp.dot(weights.astype(jnp.bfloat16), head_v, preferred_element_type=jnp.float32) / total

    def one_group(inputs):
        group_q, group_k, group_v = inputs
        all_keys = jnp.concatenate([group_k, ref_keys], axis=1)
        all_values = jnp.concatenate([group_v, ref_values], axis=1)
        return lax.map(one_head, (group_q, all_keys, all_values))
    result = lax.map(one_group, (q_groups, k_groups, v_groups))
    return result.transpose(0, 2, 1, 3).reshape(TOKENS, WIDTH).astype(jnp.bfloat16)
```

```python
import jax
import jax.numpy as jnp
from jax import lax
from jax.experimental import pallas as pl
from jax.experimental.pallas import tpu as pltpu
from jax.sharding import Mesh, PartitionSpec as P

HEADS = 40
HEAD_DIM = 128
WIDTH = HEADS * HEAD_DIM
BLK = 4
ULY = 8
PEERS = BLK * ULY
TOKENS = 16
QUARTER = TOKENS // BLK
COLUMN = 8
ROWS = TOKENS + 8
SHARED_ROW = 3 * TOKENS
REF_ROW = SHARED_ROW + 3 * QUARTER
ALL_SETS = (REF_ROW + 8) // QUARTER
PAIR = 2 * HEAD_DIM
VMEM_LIMIT = 48 * 1024 * 1024
PARAMS = pltpu.CompilerParams(vmem_limit_bytes=VMEM_LIMIT)
WHOLE_VMEM = pltpu.CompilerParams(vmem_limit_bytes=60 * 1024 * 1024)
VMEM = pl.BlockSpec(memory_space=pltpu.VMEM)
ANY = pl.BlockSpec(memory_space=pl.ANY)
HBM = pl.BlockSpec(memory_space=pltpu.HBM)


def lanes(index, width=HEAD_DIM):
    return slice(index * width, (index + 1) * width)


def peers():
    for blk in range(BLK):
        for uly in range(ULY):
            yield blk * ULY + uly, blk, BLK * uly + blk, PEERS + uly


def rotary_tables(position):
    pairs = HEAD_DIM // 2
    side = HEAD_DIM // 6
    time = pairs - 2 * side
    eye = lax.broadcasted_iota(jnp.int32, (TOKENS, TOKENS), 0) == lax.broadcasted_iota(
        jnp.int32, (TOKENS, TOKENS), 1
    )
    columns = [
        jnp.sum(jnp.where(eye, position[axis : axis + 1, :], 0.0), axis=1, keepdims=True)
        for axis in range(3)
    ]
    lane = lax.broadcasted_iota(jnp.int32, (TOKENS, HEAD_DIM), 1)
    pair = lax.shift_right_logical(lane, 1)
    in_time = pair < time
    in_row = pair < time + side
    local = (pair - jnp.where(in_time, 0, jnp.where(in_row, time, time + side))).astype(jnp.float32)
    number = jnp.where(in_time, float(time), float(side))
    frequency = jnp.exp(local / number * -9.210340371976184)
    angle = jnp.where(in_time, columns[0], jnp.where(in_row, columns[1], columns[2])) * frequency
    return jnp.cos(angle), jnp.sin(angle), lax.rem(lane, 2) == 0


def inverse_rms(source_ref):
    wide = source_ref[...].astype(jnp.float32)
    return lax.rsqrt(jnp.mean(wide * wide, axis=1, keepdims=True) + 1e-06)


def rotation(pos_ref):
    cos, sin, even = rotary_tables(pos_ref[...].astype(jnp.float32))
    return cos, jnp.where(even, -sin, 0.0), jnp.where(even, 0.0, sin)


def turn(source_ref, gain_ref, head, scale, tables):
    cos, sin_next, sin_prev = tables
    normed = source_ref[:, lanes(head)].astype(jnp.float32) * scale * gain_ref[:, lanes(head)]
    turned = (
        normed * cos
        + pltpu.roll(normed, HEAD_DIM - 1, 1) * sin_next
        + pltpu.roll(normed, 1, 1) * sin_prev
    )
    return turned.astype(jnp.bfloat16)


def spread(out_ref, head, block, main_row, shared_row):
    for peer, blk, whole, shared in peers():
        if head == whole:
            out_ref[peer, main_row : main_row + TOKENS, :] = block
        if head == shared:
            out_ref[peer, shared_row : shared_row + QUARTER, :] = block[
                QUARTER * blk : QUARTER * (blk + 1), :
            ]


def start_all(pairs, sems):
    copies = [
        pltpu.make_async_copy(source, target, sems.at[index])
        for index, (source, target) in enumerate(pairs)
    ]
    for copy in copies:
        copy.start()
    return copies


WIDE = pltpu.VMEM((TOKENS, WIDTH), jnp.bfloat16)
GAIN = pltpu.VMEM((1, WIDTH), jnp.float32)
PLACES = pltpu.VMEM((3, TOKENS), jnp.int32)


def pieces_kernel(
    k_hbm, v_hbm, gk_hbm, pos_hbm, group_hbm, ref_out, place_out,
    k_ref, v_ref, gk_ref, pos_ref, group_ref, sems,
):
    pairs = [
        (pos_hbm, pos_ref), (k_hbm, k_ref), (gk_hbm, gk_ref),
        (v_hbm, v_ref), (group_hbm, group_ref),
    ]
    copies = start_all(pairs, sems)

    def share(head, block, half):
        for piece in range(COLUMN):
            ref_out[piece, :, lanes(2 * head + half)] = block[2 * piece : 2 * piece + 2, :]

    copies[0].wait()
    tables = rotation(pos_ref)
    copies[1].wait()
    copies[2].wait()
    scale = inverse_rms(k_ref)
    for head in range(HEADS):
        share(head, turn(k_ref, gk_ref, head, scale, tables), 0)
    copies[3].wait()
    for head in range(HEADS):
        share(head, v_ref[:, lanes(head)], 1)
    copies[4].wait()
    group = group_ref[...]
    ids = lax.broadcasted_iota(jnp.int32, group.shape, 1)
    root = jnp.sum(jnp.where(group == 0, ids, 0), axis=1, keepdims=True)
    source = 2 * lax.shift_right_logical(root, 2) + jnp.bitwise_and(root, 1)
    half = jnp.bitwise_and(lax.shift_right_logical(root, 1) + lax.axis_index("half"), 1)
    lane = lax.broadcasted_iota(jnp.int32, place_out.shape, 1)
    place_out[...] = jnp.where(lane == 0, source, half)


def make_pieces(keys, values, gain_k, positions, ref_group):
    return pl.pallas_call(
        pieces_kernel,
        in_specs=[HBM] * 5,
        out_specs=(VMEM,) * 2,
        out_shape=(
            jax.ShapeDtypeStruct((COLUMN, 2, HEADS * PAIR), jnp.bfloat16),
            jax.ShapeDtypeStruct((8, HEAD_DIM), jnp.int32),
        ),
        scratch_shapes=[
            WIDE, WIDE, GAIN, PLACES,
            pltpu.VMEM((1, 16), jnp.int32),
            pltpu.SemaphoreType.DMA((5,)),
        ],
        compiler_params=WHOLE_VMEM,
        name="reference_pieces",
    )(keys, values, gain_k.reshape(1, WIDTH), positions, ref_group.reshape(1, 16))


def blocks_kernel(
    q_hbm, k_hbm, v_hbm, gq_hbm, gk_hbm, pos_hbm, out_ref,
    q_ref, k_ref, v_ref, gq_ref, gk_ref, pos_ref, sems,
):
    pairs = [
        (pos_hbm, pos_ref), (k_hbm, k_ref), (gk_hbm, gk_ref),
        (v_hbm, v_ref), (q_hbm, q_ref), (gq_hbm, gq_ref),
    ]
    copies = start_all(pairs, sems)

    def place(head, block, part):
        spread(out_ref, head, block, TOKENS * part, SHARED_ROW + QUARTER * part)

    copies[0].wait()
    tables = rotation(pos_ref)
    copies[1].wait()
    copies[2].wait()
    scale = inverse_rms(k_ref)
    for head in range(HEADS):
        place(head, turn(k_ref, gk_ref, head, scale, tables), 0)
    copies[3].wait()
    for head in range(HEADS):
        place(head, v_ref[:, lanes(head)], 1)
    copies[4].wait()
    copies[5].wait()
    scale = inverse_rms(q_ref)
    for head in range(HEADS):
        place(head, turn(q_ref, gq_ref, head, scale, tables), 2)


def make_blocks(queries, keys, values, gain_q, gain_k, positions):
    return pl.pallas_call(
        blocks_kernel,
        in_specs=[HBM] * 6,
        out_specs=VMEM,
        out_shape=jax.ShapeDtypeStruct((PEERS, REF_ROW + 4, HEAD_DIM), jnp.bfloat16),
        scratch_shapes=[WIDE, WIDE, WIDE, GAIN, GAIN, PLACES, pltpu.SemaphoreType.DMA((6,))],
        compiler_params=PARAMS,
        name="exchange_blocks",
    )(queries, keys, values, gain_q.reshape(1, WIDTH), gain_k.reshape(1, WIDTH), positions)


def pick_kernel(place_ref, scattered_ref, out_ref):
    out_ref[...] = scattered_ref[place_ref[0, 0]]


def pick(place, scattered):
    return pl.pallas_call(
        pick_kernel,
        in_specs=[VMEM, VMEM],
        out_specs=VMEM,
        out_shape=jax.ShapeDtypeStruct((2, HEADS * PAIR), jnp.bfloat16),
        compiler_params=PARAMS,
        name="pick_reference",
    )(place, scattered)


def insert_kernel(place_ref, own_ref, other_ref, blocks_ref, out_ref):
    for index in range(REF_ROW // QUARTER):
        out_ref[:, index, :, :] = blocks_ref[:, QUARTER * index : QUARTER * (index + 1), :]

    def put(source_ref):
        for peer, _, whole, shared in peers():
            columns = (2 * whole, 2 * whole + 1, 2 * shared, 2 * shared + 1)
            for part, column in enumerate(columns):
                index, row = REF_ROW // QUARTER + part // 2, 2 * (part % 2)
                out_ref[peer, index, row : row + 2, :] = source_ref[:, lanes(column)]

    other = place_ref[0, 1] == 1

    @pl.when(other)
    def _():
        put(other_ref)

    @pl.when(jnp.logical_not(other))
    def _():
        put(own_ref)


def insert(place, own, other, blocks):
    return pl.pallas_call(
        insert_kernel,
        in_specs=[VMEM] * 4,
        out_specs=VMEM,
        out_shape=jax.ShapeDtypeStruct((PEERS, ALL_SETS, QUARTER, HEAD_DIM), jnp.bfloat16),
        compiler_params=PARAMS,
        name="insert_reference",
    )(place, own, other, blocks)


def flatten_kernel(got_ref, out_ref):
    for peer in range(PEERS):
        for part in range(4):
            target = 2 * PEERS * part + 2 * peer
            index, row = REF_ROW // QUARTER + part // 2, 2 * (part % 2)
            out_ref[0, target : target + 2, :] = got_ref[peer, index, row : row + 2, :]
    for copy in range(1, COLUMN):
        out_ref[copy] = out_ref[0]


def flatten(got):
    return pl.pallas_call(
        flatten_kernel,
        in_specs=[VMEM],
        out_specs=VMEM,
        out_shape=jax.ShapeDtypeStruct((COLUMN, 8 * PEERS, HEAD_DIM), jnp.bfloat16),
        compiler_params=PARAMS,
        name="flatten_reference",
    )(got)


def compact_kernel(got_ref, out_ref):
    for peer in range(PEERS):
        for part in range(2):
            target = PEERS * QUARTER * part + QUARTER * peer
            out_ref[target : target + QUARTER, :] = got_ref[peer, SHARED_ROW // QUARTER + part]


def compact(got):
    return pl.pallas_call(
        compact_kernel,
        in_specs=[VMEM],
        out_specs=VMEM,
        out_shape=jax.ShapeDtypeStruct((2 * PEERS * QUARTER, HEAD_DIM), jnp.bfloat16),
        compiler_params=PARAMS,
        name="shared_head",
    )(got)


def attend_kernel(got_ref, fifth_ref, ref_ref, out_ref, shared_q):
    exponent_scale = HEAD_DIM ** (-0.5) * 1.4426950408889634

    def scores(queried, keyed):
        return lax.dot_general(
            queried, keyed, (((1,), (1,)), ((), ())), preferred_element_type=jnp.float32
        )

    def attention(queried, key_a, value_a, key_b, value_b):
        scores_a = scores(queried, key_a)
        scores_b = scores(queried, key_b)
        largest = jnp.maximum(
            jnp.max(scores_a, axis=1, keepdims=True), jnp.max(scores_b, axis=1, keepdims=True)
        )
        weights_a = jnp.exp2((scores_a - largest) * exponent_scale)
        weights_b = jnp.exp2((scores_b - largest) * exponent_scale)
        total = jnp.sum(weights_a, axis=1, keepdims=True) + jnp.sum(
            weights_b, axis=1, keepdims=True
        )
        mixed = jnp.dot(
            weights_a.astype(jnp.bfloat16), value_a, preferred_element_type=jnp.float32
        ) + jnp.dot(weights_b.astype(jnp.bfloat16), value_b, preferred_element_type=jnp.float32)
        return (mixed / total).astype(jnp.bfloat16)

    def part(source_ref, index, height):
        return source_ref[:, height * index : height * (index + 1), :].reshape(-1, HEAD_DIM)

    def own(index):
        sets = TOKENS // QUARTER
        return got_ref[:, sets * index : sets * (index + 1), :, :].reshape(-1, HEAD_DIM)

    key_own, value_own = own(0), own(1)
    key_ref, value_ref = part(ref_ref, 0, 64), part(ref_ref, 1, 64)
    out_ref[:, 0:TOKENS, :] = attention(own(2), key_own, value_own, key_ref, value_ref).reshape(
        PEERS, TOKENS, HEAD_DIM
    )
    for peer in range(PEERS):
        shared_q[QUARTER * peer : QUARTER * (peer + 1), :] = got_ref[
            peer, SHARED_ROW // QUARTER + 2
        ]
    shared = attention(
        shared_q[...],
        part(fifth_ref, 0, 128),
        part(fifth_ref, 1, 128),
        part(ref_ref, 2, 64),
        part(ref_ref, 3, 64),
    )
    for peer in range(PEERS):
        out_ref[peer, TOKENS : TOKENS + QUARTER, :] = shared[
            QUARTER * peer : QUARTER * (peer + 1), :
        ]


def attend(got, fifth, ref):
    return pl.pallas_call(
        attend_kernel,
        in_specs=[VMEM] * 3,
        out_specs=VMEM,
        out_shape=jax.ShapeDtypeStruct((PEERS, ROWS, HEAD_DIM), jnp.bfloat16),
        scratch_shapes=[pltpu.VMEM((PEERS * QUARTER, HEAD_DIM), jnp.bfloat16)],
        compiler_params=PARAMS,
        name="attention",
    )(got, fifth, ref)


def assemble_kernel(got_ref, out_hbm, whole_ref, sem):
    for peer, blk, whole, shared in peers():
        whole_ref[:, lanes(whole)] = got_ref[peer, 0:TOKENS, :]
        whole_ref[QUARTER * blk : QUARTER * (blk + 1), lanes(shared)] = got_ref[
            peer, TOKENS : TOKENS + QUARTER, :
        ]
    copy = pltpu.make_async_copy(whole_ref, out_hbm, sem)
    copy.start()
    copy.wait()


def assemble(got):
    return pl.pallas_call(
        assemble_kernel,
        in_specs=[VMEM],
        out_specs=HBM,
        out_shape=jax.ShapeDtypeStruct((TOKENS, WIDTH), jnp.bfloat16),
        scratch_shapes=[pltpu.VMEM((TOKENS, WIDTH), jnp.bfloat16), pltpu.SemaphoreType.DMA],
        compiler_params=PARAMS,
        name="assemble",
    )(got)


def local(queries, keys, values, gain_q, gain_k, positions, ref_group):
    pieces, place = make_pieces(keys, values, gain_k, positions, ref_group)
    own = pick(place, lax.all_to_all(pieces, ("x", "core"), 0, 0, tiled=True))
    swap = [
        (half * ULY + uly, (1 - half) * ULY + (uly + ULY // 2) % ULY)
        for half in range(2)
        for uly in range(ULY)
    ]
    other = lax.ppermute(own, ("half", "uly"), swap)
    blocks = make_blocks(queries, keys, values, gain_q, gain_k, positions)
    packed = insert(place, own, other, blocks)
    got = lax.all_to_all(packed, ("blk", "uly"), 0, 0, tiled=True)

    ref = lax.all_to_all(flatten(got), ("x", "core"), 0, 0, tiled=True)
    fifth = lax.all_gather(compact(got), "blk", axis=0, tiled=False)

    attended = attend(got, fifth, ref)
    return assemble(lax.all_to_all(attended, ("blk", "uly"), 0, 0, tiled=True))


def solution(mesh):
    rows = ("x", "half", "core", "blk", "uly")
    fine = Mesh(mesh.devices.reshape(4, 2, 2, BLK, ULY), rows)
    whole, split = P(), P(rows, None)
    in_specs = (split, split, split, whole, whole, P(None, rows), whole)
    return jax.shard_map(local, mesh=fine, in_specs=in_specs, out_specs=split, check_vma=False)
```

```python
import jax
import jax.numpy as jnp
from jax import lax
from jax.experimental import pallas as pl
from jax.experimental.pallas import tpu as pltpu
from jax.sharding import Mesh, PartitionSpec as P

HEADS = 40
HEAD_DIM = 128
WIDTH = HEADS * HEAD_DIM
BLK = 4
ULY = 8
PEERS = BLK * ULY
TOKENS = 16
QUARTER = TOKENS // BLK
COLUMN = 8
ROWS = TOKENS + 8
SHARED_ROW = 3 * TOKENS
REF_ROW = SHARED_ROW + 3 * QUARTER
ALL_SETS = (REF_ROW + 8) // QUARTER
PAIR = 2 * HEAD_DIM
VMEM_LIMIT = 48 * 1024 * 1024
PARAMS = pltpu.CompilerParams(vmem_limit_bytes=VMEM_LIMIT)
WHOLE_VMEM = pltpu.CompilerParams(vmem_limit_bytes=60 * 1024 * 1024)
VMEM = pl.BlockSpec(memory_space=pltpu.VMEM)
ANY = pl.BlockSpec(memory_space=pl.ANY)
HBM = pl.BlockSpec(memory_space=pltpu.HBM)


def lanes(index, width=HEAD_DIM):
    return slice(index * width, (index + 1) * width)


def peers():
    for blk in range(BLK):
        for uly in range(ULY):
            yield blk * ULY + uly, blk, BLK * uly + blk, PEERS + uly


def rotary_tables(position):
    pairs = HEAD_DIM // 2
    side = HEAD_DIM // 6
    time = pairs - 2 * side
    eye = lax.broadcasted_iota(jnp.int32, (TOKENS, TOKENS), 0) == lax.broadcasted_iota(
        jnp.int32, (TOKENS, TOKENS), 1
    )
    columns = [
        jnp.sum(jnp.where(eye, position[axis : axis + 1, :], 0.0), axis=1, keepdims=True)
        for axis in range(3)
    ]
    lane = lax.broadcasted_iota(jnp.int32, (TOKENS, HEAD_DIM), 1)
    pair = lax.shift_right_logical(lane, 1)
    in_time = pair < time
    in_row = pair < time + side
    local = (pair - jnp.where(in_time, 0, jnp.where(in_row, time, time + side))).astype(jnp.float32)
    number = jnp.where(in_time, float(time), float(side))
    frequency = jnp.exp(local / number * -9.210340371976184)
    angle = jnp.where(in_time, columns[0], jnp.where(in_row, columns[1], columns[2])) * frequency
    return jnp.cos(angle), jnp.sin(angle), lax.rem(lane, 2) == 0


def inverse_rms(source_ref):
    wide = source_ref[...].astype(jnp.float32)
    return lax.rsqrt(jnp.mean(wide * wide, axis=1, keepdims=True) + 1e-06)


def rotation(pos_ref):
    cos, sin, even = rotary_tables(pos_ref[...].astype(jnp.float32))
    return cos, jnp.where(even, -sin, 0.0), jnp.where(even, 0.0, sin)


def turn(source_ref, gain_ref, head, scale, tables):
    cos, sin_next, sin_prev = tables
    normed = source_ref[:, lanes(head)].astype(jnp.float32) * scale * gain_ref[:, lanes(head)]
    turned = (
        normed * cos
        + pltpu.roll(normed, HEAD_DIM - 1, 1) * sin_next
        + pltpu.roll(normed, 1, 1) * sin_prev
    )
    return turned.astype(jnp.bfloat16)


def spread(out_ref, head, block, main_row, shared_row):
    for peer, blk, whole, shared in peers():
        if head == whole:
            out_ref[peer, main_row : main_row + TOKENS, :] = block
        if head == shared:
            out_ref[peer, shared_row : shared_row + QUARTER, :] = block[
                QUARTER * blk : QUARTER * (blk + 1), :
            ]


def start_all(pairs, sems):
    copies = [
        pltpu.make_async_copy(source, target, sems.at[index])
        for index, (source, target) in enumerate(pairs)
    ]
    for copy in copies:
        copy.start()
    return copies


WIDE = pltpu.VMEM((TOKENS, WIDTH), jnp.bfloat16)
GAIN = pltpu.VMEM((1, WIDTH), jnp.float32)
PLACES = pltpu.VMEM((3, TOKENS), jnp.int32)


def pieces_kernel(
    k_hbm, v_hbm, gk_hbm, pos_hbm, group_hbm, ref_out, place_out,
    k_ref, v_ref, gk_ref, pos_ref, group_ref, sems,
):
    pairs = [
        (pos_hbm, pos_ref), (k_hbm, k_ref), (gk_hbm, gk_ref),
        (v_hbm, v_ref), (group_hbm, group_ref),
    ]
    copies = start_all(pairs, sems)

    def share(head, block, half):
        for piece in range(COLUMN):
            ref_out[piece, :, lanes(2 * head + half)] = block[2 * piece : 2 * piece + 2, :]

    copies[0].wait()
    tables = rotation(pos_ref)
    copies[1].wait()
    copies[2].wait()
    scale = inverse_rms(k_ref)
    for head in range(HEADS):
        share(head, turn(k_ref, gk_ref, head, scale, tables), 0)
    copies[3].wait()
    for head in range(HEADS):
        share(head, v_ref[:, lanes(head)], 1)
    copies[4].wait()
    group = group_ref[...]
    ids = lax.broadcasted_iota(jnp.int32, group.shape, 1)
    root = jnp.sum(jnp.where(group == 0, ids, 0), axis=1, keepdims=True)
    source = 2 * lax.shift_right_logical(root, 2) + jnp.bitwise_and(root, 1)
    half = jnp.bitwise_and(lax.shift_right_logical(root, 1) + lax.axis_index("half"), 1)
    lane = lax.broadcasted_iota(jnp.int32, place_out.shape, 1)
    place_out[...] = jnp.where(lane == 0, source, half)


def make_pieces(keys, values, gain_k, positions, ref_group):
    return pl.pallas_call(
        pieces_kernel,
        in_specs=[HBM] * 5,
        out_specs=(VMEM,) * 2,
        out_shape=(
            jax.ShapeDtypeStruct((COLUMN, 2, HEADS * PAIR), jnp.bfloat16),
            jax.ShapeDtypeStruct((8, HEAD_DIM), jnp.int32),
        ),
        scratch_shapes=[
            WIDE, WIDE, GAIN, PLACES,
            pltpu.VMEM((1, 16), jnp.int32),
            pltpu.SemaphoreType.DMA((5,)),
        ],
        compiler_params=WHOLE_VMEM,
        name="reference_pieces",
    )(keys, values, gain_k.reshape(1, WIDTH), positions, ref_group.reshape(1, 16))


def blocks_kernel(
    q_hbm, k_hbm, v_hbm, gq_hbm, gk_hbm, pos_hbm, out_ref,
    q_ref, k_ref, v_ref, gq_ref, gk_ref, pos_ref, sems,
):
    pairs = [
        (pos_hbm, pos_ref), (k_hbm, k_ref), (gk_hbm, gk_ref),
        (v_hbm, v_ref), (q_hbm, q_ref), (gq_hbm, gq_ref),
    ]
    copies = start_all(pairs, sems)

    def place(head, block, part):
        spread(out_ref, head, block, TOKENS * part, SHARED_ROW + QUARTER * part)

    copies[0].wait()
    tables = rotation(pos_ref)
    copies[1].wait()
    copies[2].wait()
    scale = inverse_rms(k_ref)
    for head in range(HEADS):
        place(head, turn(k_ref, gk_ref, head, scale, tables), 0)
    copies[3].wait()
    for head in range(HEADS):
        place(head, v_ref[:, lanes(head)], 1)
    copies[4].wait()
    copies[5].wait()
    scale = inverse_rms(q_ref)
    for head in range(HEADS):
        place(head, turn(q_ref, gq_ref, head, scale, tables), 2)


def make_blocks(queries, keys, values, gain_q, gain_k, positions):
    return pl.pallas_call(
        blocks_kernel,
        in_specs=[HBM] * 6,
        out_specs=VMEM,
        out_shape=jax.ShapeDtypeStruct((PEERS, REF_ROW + 4, HEAD_DIM), jnp.bfloat16),
        scratch_shapes=[WIDE, WIDE, WIDE, GAIN, GAIN, PLACES, pltpu.SemaphoreType.DMA((6,))],
        compiler_params=PARAMS,
        name="exchange_blocks",
    )(queries, keys, values, gain_q.reshape(1, WIDTH), gain_k.reshape(1, WIDTH), positions)


def pick_kernel(place_ref, scattered_ref, out_ref):
    out_ref[...] = scattered_ref[place_ref[0, 0]]


def pick(place, scattered):
    return pl.pallas_call(
        pick_kernel,
        in_specs=[VMEM, VMEM],
        out_specs=VMEM,
        out_shape=jax.ShapeDtypeStruct((2, HEADS * PAIR), jnp.bfloat16),
        compiler_params=PARAMS,
        name="pick_reference",
    )(place, scattered)


def insert_kernel(place_ref, own_ref, other_ref, blocks_ref, out_ref):
    for index in range(REF_ROW // QUARTER):
        out_ref[:, index, :, :] = blocks_ref[:, QUARTER * index : QUARTER * (index + 1), :]

    def put(source_ref):
        for peer, _, whole, shared in peers():
            columns = (2 * whole, 2 * whole + 1, 2 * shared, 2 * shared + 1)
            for part, column in enumerate(columns):
                index, row = REF_ROW // QUARTER + part // 2, 2 * (part % 2)
                out_ref[peer, index, row : row + 2, :] = source_ref[:, lanes(column)]

    other = place_ref[0, 1] == 1

    @pl.when(other)
    def _():
        put(other_ref)

    @pl.when(jnp.logical_not(other))
    def _():
        put(own_ref)


def insert(place, own, other, blocks):
    return pl.pallas_call(
        insert_kernel,
        in_specs=[VMEM] * 4,
        out_specs=VMEM,
        out_shape=jax.ShapeDtypeStruct((PEERS, ALL_SETS, QUARTER, HEAD_DIM), jnp.bfloat16),
        compiler_params=PARAMS,
        name="insert_reference",
    )(place, own, other, blocks)


def flatten_kernel(got_ref, out_hbm, flat_ref, sems):
    for peer in range(PEERS):
        for part in range(4):
            target = 2 * PEERS * part + 2 * peer
            index, row = REF_ROW // QUARTER + part // 2, 2 * (part % 2)
            flat_ref[target : target + 2, :] = got_ref[peer, index, row : row + 2, :]
    copies = start_all([(flat_ref, out_hbm.at[copy]) for copy in range(COLUMN)], sems)
    for copy in copies:
        copy.wait()


def flatten(got):
    return pl.pallas_call(
        flatten_kernel,
        in_specs=[VMEM],
        out_specs=HBM,
        out_shape=jax.ShapeDtypeStruct((COLUMN, 8 * PEERS, HEAD_DIM), jnp.bfloat16),
        scratch_shapes=[
            pltpu.VMEM((8 * PEERS, HEAD_DIM), jnp.bfloat16),
            pltpu.SemaphoreType.DMA((COLUMN,)),
        ],
        compiler_params=PARAMS,
        name="flatten_reference",
    )(got)


def compact_kernel(got_ref, out_ref):
    for peer in range(PEERS):
        for part in range(2):
            target = PEERS * QUARTER * part + QUARTER * peer
            out_ref[target : target + QUARTER, :] = got_ref[peer, SHARED_ROW // QUARTER + part]


def compact(got):
    return pl.pallas_call(
        compact_kernel,
        in_specs=[VMEM],
        out_specs=VMEM,
        out_shape=jax.ShapeDtypeStruct((2 * PEERS * QUARTER, HEAD_DIM), jnp.bfloat16),
        compiler_params=PARAMS,
        name="shared_head",
    )(got)


def attend_kernel(got_ref, fifth_ref, ref_ref, out_ref, shared_q):
    exponent_scale = HEAD_DIM ** (-0.5) * 1.4426950408889634

    def scores(queried, keyed):
        return lax.dot_general(
            queried, keyed, (((1,), (1,)), ((), ())), preferred_element_type=jnp.float32
        )

    def attention(queried, key_a, value_a, key_b, value_b):
        scores_a = scores(queried, key_a)
        scores_b = scores(queried, key_b)
        largest = jnp.maximum(
            jnp.max(scores_a, axis=1, keepdims=True), jnp.max(scores_b, axis=1, keepdims=True)
        )
        weights_a = jnp.exp2((scores_a - largest) * exponent_scale)
        weights_b = jnp.exp2((scores_b - largest) * exponent_scale)
        total = jnp.sum(weights_a, axis=1, keepdims=True) + jnp.sum(
            weights_b, axis=1, keepdims=True
        )
        mixed = jnp.dot(
            weights_a.astype(jnp.bfloat16), value_a, preferred_element_type=jnp.float32
        ) + jnp.dot(weights_b.astype(jnp.bfloat16), value_b, preferred_element_type=jnp.float32)
        return (mixed / total).astype(jnp.bfloat16)

    def part(source_ref, index, height):
        return source_ref[:, height * index : height * (index + 1), :].reshape(-1, HEAD_DIM)

    def own(index):
        sets = TOKENS // QUARTER
        return got_ref[:, sets * index : sets * (index + 1), :, :].reshape(-1, HEAD_DIM)

    key_own, value_own = own(0), own(1)
    key_ref, value_ref = part(ref_ref, 0, 64), part(ref_ref, 1, 64)
    sets = TOKENS // QUARTER
    out_ref[:, 0:sets, :, :] = attention(own(2), key_own, value_own, key_ref, value_ref).reshape(
        PEERS, sets, QUARTER, HEAD_DIM
    )
    for peer in range(PEERS):
        shared_q[QUARTER * peer : QUARTER * (peer + 1), :] = got_ref[
            peer, SHARED_ROW // QUARTER + 2
        ]
    shared = attention(
        shared_q[...],
        part(fifth_ref, 0, 128),
        part(fifth_ref, 1, 128),
        part(ref_ref, 2, 64),
        part(ref_ref, 3, 64),
    )
    for peer in range(PEERS):
        out_ref[peer, sets, :, :] = shared[QUARTER * peer : QUARTER * (peer + 1), :]


def attend(got, fifth, ref):
    return pl.pallas_call(
        attend_kernel,
        in_specs=[VMEM] * 3,
        out_specs=VMEM,
        out_shape=jax.ShapeDtypeStruct((PEERS, TOKENS // QUARTER + 1, QUARTER, HEAD_DIM), jnp.bfloat16),
        scratch_shapes=[pltpu.VMEM((PEERS * QUARTER, HEAD_DIM), jnp.bfloat16)],
        compiler_params=PARAMS,
        name="attention",
    )(got, fifth, ref)


def assemble_kernel(got_ref, out_hbm, whole_ref, sem):
    for peer, blk, whole, shared in peers():
        sets = TOKENS // QUARTER
        whole_ref[:, lanes(whole)] = got_ref[peer, 0:sets].reshape(TOKENS, HEAD_DIM)
        whole_ref[QUARTER * blk : QUARTER * (blk + 1), lanes(shared)] = got_ref[peer, sets]
    copy = pltpu.make_async_copy(whole_ref, out_hbm, sem)
    copy.start()
    copy.wait()


def assemble(got):
    return pl.pallas_call(
        assemble_kernel,
        in_specs=[VMEM],
        out_specs=HBM,
        out_shape=jax.ShapeDtypeStruct((TOKENS, WIDTH), jnp.bfloat16),
        scratch_shapes=[pltpu.VMEM((TOKENS, WIDTH), jnp.bfloat16), pltpu.SemaphoreType.DMA],
        compiler_params=PARAMS,
        name="assemble",
    )(got)


def local(queries, keys, values, gain_q, gain_k, positions, ref_group):
    pieces, place = make_pieces(keys, values, gain_k, positions, ref_group)
    own = pick(place, lax.all_to_all(pieces, ("x", "core"), 0, 0, tiled=True))
    swap = [
        (half * ULY + uly, (1 - half) * ULY + (uly + ULY // 2) % ULY)
        for half in range(2)
        for uly in range(ULY)
    ]
    other = lax.ppermute(own, ("half", "uly"), swap)
    blocks = make_blocks(queries, keys, values, gain_q, gain_k, positions)
    packed = insert(place, own, other, blocks)
    got = lax.all_to_all(packed, ("blk", "uly"), 0, 0, tiled=True)

    ref = lax.all_to_all(flatten(got), ("x", "core"), 0, 0, tiled=True)
    fifth = lax.all_gather(compact(got), "blk", axis=0, tiled=False)

    attended = attend(got, fifth, ref)
    return assemble(lax.all_to_all(attended, ("blk", "uly"), 0, 0, tiled=True))


def solution(mesh):
    rows = ("x", "half", "core", "blk", "uly")
    fine = Mesh(mesh.devices.reshape(4, 2, 2, BLK, ULY), rows)
    whole, split = P(), P(rows, None)
    in_specs = (split, split, split, whole, whole, P(None, rows), whole)
    return jax.shard_map(local, mesh=fine, in_specs=in_specs, out_specs=split, check_vma=False)
```

```python
import jax
import jax.numpy as jnp
from jax import lax
from jax.experimental import pallas as pl
from jax.experimental.pallas import tpu as pltpu
from jax.sharding import Mesh, PartitionSpec as P

HEADS = 40
HEAD_DIM = 128
WIDTH = HEADS * HEAD_DIM
BLK = 4
ULY = 8
PEERS = BLK * ULY
TOKENS = 16
QUARTER = TOKENS // BLK
COLUMN = 8
ROWS = TOKENS + 8
SHARED_ROW = 3 * TOKENS
REF_ROW = SHARED_ROW + 3 * QUARTER
ALL_SETS = (REF_ROW + 8) // QUARTER
PAIR = 2 * HEAD_DIM
VMEM_LIMIT = 48 * 1024 * 1024
PARAMS = pltpu.CompilerParams(vmem_limit_bytes=VMEM_LIMIT)
WHOLE_VMEM = pltpu.CompilerParams(vmem_limit_bytes=60 * 1024 * 1024)
VMEM = pl.BlockSpec(memory_space=pltpu.VMEM)
ANY = pl.BlockSpec(memory_space=pl.ANY)
HBM = pl.BlockSpec(memory_space=pltpu.HBM)


def lanes(index, width=HEAD_DIM):
    return slice(index * width, (index + 1) * width)


def peers():
    for blk in range(BLK):
        for uly in range(ULY):
            yield blk * ULY + uly, blk, BLK * uly + blk, PEERS + uly


def rotary_tables(position):
    pairs = HEAD_DIM // 2
    side = HEAD_DIM // 6
    time = pairs - 2 * side
    eye = lax.broadcasted_iota(jnp.int32, (TOKENS, TOKENS), 0) == lax.broadcasted_iota(
        jnp.int32, (TOKENS, TOKENS), 1
    )
    columns = [
        jnp.sum(jnp.where(eye, position[axis : axis + 1, :], 0.0), axis=1, keepdims=True)
        for axis in range(3)
    ]
    lane = lax.broadcasted_iota(jnp.int32, (TOKENS, HEAD_DIM), 1)
    pair = lax.shift_right_logical(lane, 1)
    in_time = pair < time
    in_row = pair < time + side
    local = (pair - jnp.where(in_time, 0, jnp.where(in_row, time, time + side))).astype(jnp.float32)
    number = jnp.where(in_time, float(time), float(side))
    frequency = jnp.exp(local / number * -9.210340371976184)
    angle = jnp.where(in_time, columns[0], jnp.where(in_row, columns[1], columns[2])) * frequency
    return jnp.cos(angle), jnp.sin(angle), lax.rem(lane, 2) == 0


def inverse_rms(source_ref):
    wide = source_ref[...].astype(jnp.float32)
    return lax.rsqrt(jnp.mean(wide * wide, axis=1, keepdims=True) + 1e-06)


def rotation(pos_ref):
    cos, sin, even = rotary_tables(pos_ref[...].astype(jnp.float32))
    return cos, jnp.where(even, -sin, 0.0), jnp.where(even, 0.0, sin)


def turn(source_ref, gain_ref, head, scale, tables):
    cos, sin_next, sin_prev = tables
    normed = source_ref[:, lanes(head)].astype(jnp.float32) * scale * gain_ref[:, lanes(head)]
    turned = (
        normed * cos
        + pltpu.roll(normed, HEAD_DIM - 1, 1) * sin_next
        + pltpu.roll(normed, 1, 1) * sin_prev
    )
    return turned.astype(jnp.bfloat16)


def spread(out_ref, head, block, main_row, shared_row):
    for peer, blk, whole, shared in peers():
        if head == whole:
            out_ref[peer, main_row : main_row + TOKENS, :] = block
        if head == shared:
            out_ref[peer, shared_row : shared_row + QUARTER, :] = block[
                QUARTER * blk : QUARTER * (blk + 1), :
            ]


def start_all(pairs, sems):
    copies = [
        pltpu.make_async_copy(source, target, sems.at[index])
        for index, (source, target) in enumerate(pairs)
    ]
    for copy in copies:
        copy.start()
    return copies


WIDE = pltpu.VMEM((TOKENS, WIDTH), jnp.bfloat16)
GAIN = pltpu.VMEM((1, WIDTH), jnp.float32)
PLACES = pltpu.VMEM((3, TOKENS), jnp.int32)


def pieces_kernel(
    k_hbm, v_hbm, gk_hbm, pos_hbm, group_hbm, ref_out, place_out,
    k_ref, v_ref, gk_ref, pos_ref, group_ref, sems,
):
    pairs = [
        (pos_hbm, pos_ref), (k_hbm, k_ref), (gk_hbm, gk_ref),
        (v_hbm, v_ref), (group_hbm, group_ref),
    ]
    copies = start_all(pairs, sems)

    def share(head, block, half):
        for piece in range(COLUMN):
            ref_out[piece, :, lanes(2 * head + half)] = block[2 * piece : 2 * piece + 2, :]

    copies[0].wait()
    tables = rotation(pos_ref)
    copies[1].wait()
    copies[2].wait()
    scale = inverse_rms(k_ref)
    for head in range(HEADS):
        share(head, turn(k_ref, gk_ref, head, scale, tables), 0)
    copies[3].wait()
    for head in range(HEADS):
        share(head, v_ref[:, lanes(head)], 1)
    copies[4].wait()
    group = group_ref[...]
    ids = lax.broadcasted_iota(jnp.int32, group.shape, 1)
    root = jnp.sum(jnp.where(group == 0, ids, 0), axis=1, keepdims=True)
    source = 2 * lax.shift_right_logical(root, 2) + jnp.bitwise_and(root, 1)
    half = jnp.bitwise_and(lax.shift_right_logical(root, 1) + lax.axis_index("half"), 1)
    lane = lax.broadcasted_iota(jnp.int32, place_out.shape, 1)
    place_out[...] = jnp.where(lane == 0, source, half)


def make_pieces(keys, values, gain_k, positions, ref_group):
    return pl.pallas_call(
        pieces_kernel,
        in_specs=[HBM] * 5,
        out_specs=(VMEM,) * 2,
        out_shape=(
            jax.ShapeDtypeStruct((COLUMN, 2, HEADS * PAIR), jnp.bfloat16),
            jax.ShapeDtypeStruct((8, HEAD_DIM), jnp.int32),
        ),
        scratch_shapes=[
            WIDE, WIDE, GAIN, PLACES,
            pltpu.VMEM((1, 16), jnp.int32),
            pltpu.SemaphoreType.DMA((5,)),
        ],
        compiler_params=WHOLE_VMEM,
        name="reference_pieces",
    )(keys, values, gain_k.reshape(1, WIDTH), positions, ref_group.reshape(1, 16))


def blocks_kernel(
    q_hbm, k_hbm, v_hbm, gq_hbm, gk_hbm, pos_hbm, out_ref,
    q_ref, k_ref, v_ref, gq_ref, gk_ref, pos_ref, sems,
):
    pairs = [
        (pos_hbm, pos_ref), (k_hbm, k_ref), (gk_hbm, gk_ref),
        (v_hbm, v_ref), (q_hbm, q_ref), (gq_hbm, gq_ref),
    ]
    copies = start_all(pairs, sems)

    def place(head, block, part):
        spread(out_ref, head, block, TOKENS * part, SHARED_ROW + QUARTER * part)

    copies[0].wait()
    tables = rotation(pos_ref)
    copies[1].wait()
    copies[2].wait()
    scale = inverse_rms(k_ref)
    for head in range(HEADS):
        place(head, turn(k_ref, gk_ref, head, scale, tables), 0)
    copies[3].wait()
    for head in range(HEADS):
        place(head, v_ref[:, lanes(head)], 1)
    copies[4].wait()
    copies[5].wait()
    scale = inverse_rms(q_ref)
    for head in range(HEADS):
        place(head, turn(q_ref, gq_ref, head, scale, tables), 2)


def make_blocks(queries, keys, values, gain_q, gain_k, positions):
    return pl.pallas_call(
        blocks_kernel,
        in_specs=[HBM] * 6,
        out_specs=VMEM,
        out_shape=jax.ShapeDtypeStruct((PEERS, REF_ROW + 4, HEAD_DIM), jnp.bfloat16),
        scratch_shapes=[WIDE, WIDE, WIDE, GAIN, GAIN, PLACES, pltpu.SemaphoreType.DMA((6,))],
        compiler_params=PARAMS,
        name="exchange_blocks",
    )(queries, keys, values, gain_q.reshape(1, WIDTH), gain_k.reshape(1, WIDTH), positions)


def pick_kernel(place_ref, scattered_ref, out_ref):
    out_ref[...] = scattered_ref[place_ref[0, 0]]


def pick(place, scattered):
    return pl.pallas_call(
        pick_kernel,
        in_specs=[VMEM, VMEM],
        out_specs=VMEM,
        out_shape=jax.ShapeDtypeStruct((2, HEADS * PAIR), jnp.bfloat16),
        compiler_params=PARAMS,
        name="pick_reference",
    )(place, scattered)


def insert_kernel(place_ref, own_ref, other_ref, blocks_ref, out_ref):
    for index in range(REF_ROW // QUARTER):
        out_ref[:, index, :, :] = blocks_ref[:, QUARTER * index : QUARTER * (index + 1), :]

    def put(source_ref):
        for peer, _, whole, shared in peers():
            columns = (2 * whole, 2 * whole + 1, 2 * shared, 2 * shared + 1)
            for part, column in enumerate(columns):
                index, row = REF_ROW // QUARTER + part // 2, 2 * (part % 2)
                out_ref[peer, index, row : row + 2, :] = source_ref[:, lanes(column)]

    other = place_ref[0, 1] == 1

    @pl.when(other)
    def _():
        put(other_ref)

    @pl.when(jnp.logical_not(other))
    def _():
        put(own_ref)


def insert(place, own, other, blocks):
    return pl.pallas_call(
        insert_kernel,
        in_specs=[VMEM] * 4,
        out_specs=VMEM,
        out_shape=jax.ShapeDtypeStruct((PEERS, ALL_SETS, QUARTER, HEAD_DIM), jnp.bfloat16),
        compiler_params=PARAMS,
        name="insert_reference",
    )(place, own, other, blocks)


def flatten_kernel(got_ref, out_hbm, flat_ref, sems):
    for peer in range(PEERS):
        for part in range(4):
            target = 2 * PEERS * part + 2 * peer
            index, row = REF_ROW // QUARTER + part // 2, 2 * (part % 2)
            flat_ref[target : target + 2, :] = got_ref[peer, index, row : row + 2, :]
    copies = start_all([(flat_ref, out_hbm.at[copy]) for copy in range(COLUMN)], sems)
    for copy in copies:
        copy.wait()


def flatten(got):
    return pl.pallas_call(
        flatten_kernel,
        in_specs=[VMEM],
        out_specs=HBM,
        out_shape=jax.ShapeDtypeStruct((COLUMN, 8 * PEERS, HEAD_DIM), jnp.bfloat16),
        scratch_shapes=[
            pltpu.VMEM((8 * PEERS, HEAD_DIM), jnp.bfloat16),
            pltpu.SemaphoreType.DMA((COLUMN,)),
        ],
        compiler_params=PARAMS,
        name="flatten_reference",
    )(got)


def compact_kernel(got_ref, out_ref):
    for peer in range(PEERS):
        for part in range(2):
            target = PEERS * QUARTER * part + QUARTER * peer
            out_ref[target : target + QUARTER, :] = got_ref[peer, SHARED_ROW // QUARTER + part]


def compact(got):
    return pl.pallas_call(
        compact_kernel,
        in_specs=[VMEM],
        out_specs=VMEM,
        out_shape=jax.ShapeDtypeStruct((2 * PEERS * QUARTER, HEAD_DIM), jnp.bfloat16),
        compiler_params=PARAMS,
        name="shared_head",
    )(got)


def attend_kernel(got_ref, fifth_ref, ref_ref, out_ref, shared_q):
    exponent_scale = HEAD_DIM ** (-0.5) * 1.4426950408889634

    def scores(queried, keyed):
        return lax.dot_general(
            queried, keyed, (((1,), (1,)), ((), ())), preferred_element_type=jnp.float32
        )

    def attention(queried, key_a, value_a, key_b, value_b):
        scores_a = scores(queried, key_a)
        scores_b = scores(queried, key_b)
        largest = jnp.maximum(
            jnp.max(scores_a, axis=1, keepdims=True), jnp.max(scores_b, axis=1, keepdims=True)
        )
        weights_a = jnp.exp2((scores_a - largest) * exponent_scale)
        weights_b = jnp.exp2((scores_b - largest) * exponent_scale)
        total = jnp.sum(weights_a, axis=1, keepdims=True) + jnp.sum(
            weights_b, axis=1, keepdims=True
        )
        mixed = jnp.dot(
            weights_a.astype(jnp.bfloat16), value_a, preferred_element_type=jnp.float32
        ) + jnp.dot(weights_b.astype(jnp.bfloat16), value_b, preferred_element_type=jnp.float32)
        return (mixed / total).astype(jnp.bfloat16)

    def part(source_ref, index, height):
        return source_ref[:, height * index : height * (index + 1), :].reshape(-1, HEAD_DIM)

    def own(index):
        sets = TOKENS // QUARTER
        return got_ref[:, sets * index : sets * (index + 1), :, :].reshape(-1, HEAD_DIM)

    key_own, value_own = own(0), own(1)
    key_ref, value_ref = part(ref_ref, 0, 64), part(ref_ref, 1, 64)
    sets = TOKENS // QUARTER
    out_ref[:, 0:sets, :, :] = attention(own(2), key_own, value_own, key_ref, value_ref).reshape(
        PEERS, sets, QUARTER, HEAD_DIM
    )
    for peer in range(PEERS):
        shared_q[QUARTER * peer : QUARTER * (peer + 1), :] = got_ref[
            peer, SHARED_ROW // QUARTER + 2
        ]
    shared = attention(
        shared_q[...],
        part(fifth_ref, 0, 128),
        part(fifth_ref, 1, 128),
        part(ref_ref, 2, 64),
        part(ref_ref, 3, 64),
    )
    for peer in range(PEERS):
        out_ref[peer, sets, :, :] = shared[QUARTER * peer : QUARTER * (peer + 1), :]


def attend(got, fifth, ref):
    return pl.pallas_call(
        attend_kernel,
        in_specs=[VMEM] * 3,
        out_specs=VMEM,
        out_shape=jax.ShapeDtypeStruct((PEERS, TOKENS // QUARTER + 1, QUARTER, HEAD_DIM), jnp.bfloat16),
        scratch_shapes=[pltpu.VMEM((PEERS * QUARTER, HEAD_DIM), jnp.bfloat16)],
        compiler_params=PARAMS,
        name="attention",
    )(got, fifth, ref)


def assemble_kernel(got_ref, out_hbm, whole_ref, sems):
    sets = TOKENS // QUARTER
    span = WIDTH // 2
    copies = []
    for half in range(2):
        for peer, blk, whole, shared in peers():
            if whole * HEAD_DIM // span == half:
                whole_ref[:, lanes(whole)] = got_ref[peer, 0:sets].reshape(TOKENS, HEAD_DIM)
            if shared * HEAD_DIM // span == half:
                whole_ref[QUARTER * blk : QUARTER * (blk + 1), lanes(shared)] = got_ref[peer, sets]
        where = lanes(half, span)
        copies.append(
            pltpu.make_async_copy(whole_ref.at[:, where], out_hbm.at[:, where], sems.at[half])
        )
        copies[half].start()
    for copy in copies:
        copy.wait()


def assemble(got):
    return pl.pallas_call(
        assemble_kernel,
        in_specs=[VMEM],
        out_specs=HBM,
        out_shape=jax.ShapeDtypeStruct((TOKENS, WIDTH), jnp.bfloat16),
        scratch_shapes=[pltpu.VMEM((TOKENS, WIDTH), jnp.bfloat16), pltpu.SemaphoreType.DMA((2,))],
        compiler_params=PARAMS,
        name="assemble",
    )(got)


def local(queries, keys, values, gain_q, gain_k, positions, ref_group):
    pieces, place = make_pieces(keys, values, gain_k, positions, ref_group)
    own = pick(place, lax.all_to_all(pieces, ("x", "core"), 0, 0, tiled=True))
    swap = [
        (half * ULY + uly, (1 - half) * ULY + (uly + ULY // 2) % ULY)
        for half in range(2)
        for uly in range(ULY)
    ]
    other = lax.ppermute(own, ("half", "uly"), swap)
    blocks = make_blocks(queries, keys, values, gain_q, gain_k, positions)
    packed = insert(place, own, other, blocks)
    got = lax.all_to_all(packed, ("blk", "uly"), 0, 0, tiled=True)

    ref = lax.all_to_all(flatten(got), ("x", "core"), 0, 0, tiled=True)
    fifth = lax.all_gather(compact(got), "blk", axis=0, tiled=False)

    attended = attend(got, fifth, ref)
    return assemble(lax.all_to_all(attended, ("blk", "uly"), 0, 0, tiled=True))


def solution(mesh):
    rows = ("x", "half", "core", "blk", "uly")
    fine = Mesh(mesh.devices.reshape(4, 2, 2, BLK, ULY), rows)
    whole, split = P(), P(rows, None)
    in_specs = (split, split, split, whole, whole, P(None, rows), whole)
    return jax.shard_map(local, mesh=fine, in_specs=in_specs, out_specs=split, check_vma=False)
```
